256 devices in a mesh: mem: 4 (over y_lo, core), lat: 16 (over y_hi, z), lon: 4 (over x).
Axes of the slice: x: 4, y: 4 (y_hi: 2, y_lo: 2; y = y_hi * 2 + y_lo), z: 8, core: 2. Of those that a mesh axis runs over, the one named last changes fastest.
Arguments:
- anomalies: bfloat16 [64, 4, 384, 768], P('mem', None, 'lat', 'lon'), may hold values from -6 to 6
- innovation: float32 [1048576], P(('mem', 'lat', 'lon')), may hold values from -6 to 6
- corner_frac: float32 [2, 1048576], P(None, ('mem', 'lat', 'lon')), may hold values from 0 to 1
- corner_cell: int32 [1048576], P(('mem', 'lat', 'lon')), may hold values from 0 to 4414, as said below
- cell_owner: int32 [1048576], P(('mem', 'lat', 'lon')), may hold values from 0 to 63, as said below
- latitude_kernel: bfloat16 [384, 384], replicated, as said below
- longitude_kernel: bfloat16 [768, 768], replicated, as said below
Outputs:
- gradient: bfloat16 [64, 4, 384, 768], P('mem', None, 'lat', 'lon')
The draws below stay inside these ranges and needn't reach their ends.
Inputs may be any that keep to these rules, and one draw needn't show every extreme that they name: corner_cell = r * 192 + c with r < 23 and c < 191, so all four corners lie in the tile. `cell_owner`: tile t is latitude band t // 4 and longitude part t % 4. The observations of one device name each tile at most 256 times; between 1 and 4 tiles exactly 256 times, one of them the same tile for every device; the other tiles' counts on that device differ by at most one. `latitude_kernel`: nonnegative. `longitude_kernel`: nonnegative.
All inputs are finite; a program needn't handle non-finite values.
Results may differ from the reference program's by a relative error of at most 0.0057.
Values may be sent and summed in bfloat16 or wider, within the bound.
A program may use at most 128 MiB of HBM per device.

```python
import math
import jax
import jax.numpy as jnp
from jax import lax

LEVELS = 4
LAT_DEV = 24
LON_DEV = 192
OBS_DEV = 4096
MEMBERS = 64
LAT = 384
LON = 768
TILES = 64
CAP = 256
HOT_TILES = 4
OBS = 1048576
N_LON = 4


def draw_cell_owner(key, part):
    key = jax.random.fold_in(key, 7)
    dense_count = min(8, TILES)
    hot_most = HOT_TILES
    dense_tiles = jax.random.permutation(jax.random.fold_in(key, 1), TILES).astype(jnp.int32)[:dense_count]

    def one_block(block_key):
        key_list = jax.random.split(block_key, 4)
        hot_count = jax.random.randint(key_list[0], (), 1, hot_most + 1)
        others = jax.random.permutation(key_list[1], dense_tiles[1:])
        ranked = jnp.concatenate([dense_tiles[:1], others])
        flags = (jnp.arange(dense_count) < hot_count).astype(jnp.int32)
        hot_mask = jnp.zeros((TILES,), jnp.int32).at[ranked].set(flags)
        shuffle = jax.random.permutation(key_list[2], TILES).astype(jnp.int32)
        scores = jnp.where(hot_mask > 0, jnp.arange(TILES, dtype=jnp.int32) - TILES, shuffle)
        sorted_tiles = jnp.argsort(scores, stable=True).astype(jnp.int32)
        row_index = jnp.arange(OBS_DEV, dtype=jnp.int32)
        rest_index = jnp.maximum(row_index - hot_count * CAP, 0)
        spread_index = hot_count + rest_index % (TILES - hot_count)
        picked = jnp.where(row_index < hot_count * CAP, row_index // CAP, spread_index)
        owners = sorted_tiles[picked]
        return owners[jax.random.permutation(key_list[3], OBS_DEV)]
    block_keys = jax.vmap(lambda block: jax.random.fold_in(key, block))(jnp.arange(OBS // OBS_DEV))
    return jax.vmap(one_block)(block_keys).reshape(-1).astype(jnp.int32)


def draw_corner_cell(key, part):
    key = jax.random.fold_in(key, 9)
    first_key, second_key = jax.random.split(key)
    row_pick = jax.random.randint(first_key, (OBS,), 0, LAT_DEV - 1)
    col_pick = jax.random.randint(second_key, (OBS,), 0, LON_DEV - 1)
    cells = (row_pick * LON_DEV + col_pick).astype(jnp.int32)
    cells = cells.at[0].set((LAT_DEV - 2) * LON_DEV + LON_DEV - 2)
    cells = cells.at[1].set(0)
    return cells.astype(jnp.int32)


def draw_latitude_kernel(key, part):
    key = jax.random.fold_in(key, 3)
    index = jnp.arange(LAT, dtype=jnp.float32)
    spacing = index[:, None] - index[None, :]
    reach = 8.0 * LAT_DEV
    factor = jax.random.uniform(key, (LAT, LAT), jnp.float32, 0.5, 1.5)
    ratio = spacing / reach
    return (jnp.exp(-0.5 * ratio * ratio) * factor / math.sqrt(reach)).astype(jnp.bfloat16)


def draw_longitude_kernel(key, part):
    key = jax.random.fold_in(key, 5)
    index = jnp.arange(LON, dtype=jnp.float32)
    spacing = jnp.abs(index[:, None] - index[None, :])
    spacing = jnp.minimum(spacing, LON - spacing)
    reach = 1.0 * LON_DEV
    factor = jax.random.uniform(key, (LON, LON), jnp.float32, 0.5, 1.5)
    ratio = spacing / reach
    return (jnp.exp(-0.5 * ratio * ratio) * factor / math.sqrt(reach)).astype(jnp.bfloat16)


def shard_levels(own_key, shape, cuts, smallest, high):
    gain, own = 1.0, jax.random.fold_in(own_key, 6)
    for axis_at, shards_of in cuts:
        heights = jnp.exp(jax.random.uniform(jax.random.fold_in(own, axis_at), (shards_of,), jnp.float32, smallest / len(cuts), high / len(cuts)))
        gain = gain * jnp.repeat(heights, shape[axis_at] // shards_of).reshape([-1 if axis == axis_at else 1 for axis in range(len(shape))])
    return gain


def scatter_about(key, dims, spread, limit, cuts=(), held_as=jnp.bfloat16):
    values = spread * jax.random.normal(key, dims, jnp.float32)
    if cuts:
        values = values * shard_levels(key, dims, cuts, -0.22, 0.18)
    return jnp.clip(values, -limit, limit).astype(held_as)


def setup_inputs(seed: int = 0) -> dict:
    streams_of = jax.random.split(jax.random.key(seed), 8)
    anomalies = scatter_about(streams_of[0], (MEMBERS, LEVELS, LAT, LON), 1.0, 6.0, ((0, 4), (2, 16), (3, 4)))
    innovation = scatter_about(streams_of[1], (OBS,), 1.0, 6.0, ((0, 256),), jnp.float32)
    corner_frac = jnp.clip(1.0 * jax.random.uniform(streams_of[2], (2, OBS), jnp.float32) ** shard_levels(streams_of[2], (2, OBS), ((1, 256),), -0.2, 0.2), 0.0, 1.0)
    corner_cell = draw_corner_cell(jax.random.fold_in(streams_of[7], 71), 0)
    cell_owner = draw_cell_owner(jax.random.fold_in(streams_of[7], 71), 0)
    latitude_kernel = draw_latitude_kernel(jax.random.fold_in(streams_of[7], 71), 0)
    longitude_kernel = draw_longitude_kernel(jax.random.fold_in(streams_of[7], 71), 0)
    return {"anomalies": anomalies, "innovation": innovation, "corner_frac": corner_frac, "corner_cell": corner_cell, "cell_owner": cell_owner, "latitude_kernel": latitude_kernel, "longitude_kernel": longitude_kernel}


def reference(anomalies, innovation, corner_frac, corner_cell, cell_owner, latitude_kernel, longitude_kernel):
    frac_row = corner_frac[0]
    frac_col = corner_frac[1]
    grid_row = (cell_owner // N_LON) * LAT_DEV + corner_cell // LON_DEV
    grid_col = (cell_owner % N_LON) * LON_DEV + corner_cell % LON_DEV
    flat_index = (grid_row * LON + grid_col).astype(jnp.int32)
    forcing = jnp.zeros((LAT * LON,), jnp.float32)
    forcing = forcing.at[flat_index].add(innovation * (1.0 - frac_row) * (1.0 - frac_col))
    forcing = forcing.at[flat_index + 1].add(innovation * (1.0 - frac_row) * frac_col)
    forcing = forcing.at[flat_index + LON].add(innovation * frac_row * (1.0 - frac_col))
    forcing = forcing.at[flat_index + LON + 1].add(innovation * frac_row * frac_col)
    forcing = forcing.reshape(LAT, LON)
    lat_wide = latitude_kernel.astype(jnp.float32)
    lon_wide = longitude_kernel.astype(jnp.float32)

    def member_gradient(member_field):
        weighted = (member_field.astype(jnp.float32) * forcing).astype(jnp.bfloat16)
        mixed = jnp.einsum("il,kij->klj", lat_wide, weighted.astype(jnp.float32)).astype(jnp.bfloat16)
        return jnp.einsum("klj,jp->klp", mixed.astype(jnp.float32), lon_wide).astype(jnp.bfloat16)

    return lax.map(member_gradient, anomalies)
```

```python
import functools

import jax
import jax.numpy as jnp
from jax import lax
from jax.experimental import pallas as pl
from jax.experimental.pallas import tpu as pltpu
from jax.sharding import PartitionSpec as P

MESH = pl.DeviceIdType.MESH
F32 = jnp.float32
BF16 = jnp.bfloat16

LEVELS, ROWS, COLS = 4, 24, 192
LAT, LON, OBS = 384, 768, 4096
HALF = LON // 2
PLANE, DEPTH, GROUP = 16, 8, 64
CHUNK = 2048
PACKED = 40


def tent_table(index, low, high, count):
    width = index.shape[1]
    low, high = low.astype(BF16), high.astype(BF16)
    rows = lax.broadcasted_iota(jnp.int32, (128, width), 0).astype(F32).astype(BF16)
    parts = []
    for base in range(0, count, 128):
        at = (index - base).astype(BF16)
        after = (index - (base - 1)).astype(BF16)
        parts.append(jnp.where(rows == at, low, jnp.where(rows == after, high, BF16(0))))
    return jnp.concatenate(parts, axis=0)


def kernel(
    anom, innov, frac, cell, owner, lat_k, lon_k, out,
    v_innov, v_frac, v_cell, v_owner, v_latk, v_lonk,
    obs, row_table, col_table, total,
    psend, precv, zsend, zrecv, forcing,
    xrecv, fsend, frecv, lat_t, weighted, gsend, grecv, out_v,
    load_sem, own_sem, out_sem,
    obs_sem, x_sem, p_sem, z_sem, f_sem, ag_send, ag_recv, core_sem, g_send, g_recv,
):
    mem, lat, lon = lax.axis_index("mem"), lax.axis_index("lat"), lax.axis_index("lon")
    core, y_lo = lax.rem(mem, 2), mem // 2
    z, y_hi = lax.rem(lat, 8), lat // 8
    q = (y_hi * 2 + y_lo) * 4 + lon
    e = y_hi * 4 + lon
    me = lat * 4 + lon
    mate = {"mem": mem + 1 - 2 * core}

    def plane_peer(p):
        y = p // 4
        return {"mem": lax.rem(y, 2) * 2 + core, "lat": (y // 2) * 8 + z, "lon": lax.rem(p, 4)}

    def z_peer(to):
        return {"lat": y_hi * 8 + to}

    def remote(src, dst, send, recv, to):
        return pltpu.make_async_remote_copy(
            src_ref=src, dst_ref=dst, send_sem=send, recv_sem=recv, device_id=to, device_id_type=MESH
        )

    loads = [
        pltpu.make_async_copy(src, dst, load_sem.at[i])
        for i, (src, dst) in enumerate(
            ((innov, v_innov), (frac, v_frac), (cell, v_cell), (owner, v_owner), (lat_k, v_latk), (lon_k, v_lonk))
        )
    ]
    for load in loads:
        load.start()
    own_x = pltpu.make_async_copy(anom.at[pl.ds(y_hi * 8, 8), lon], xrecv.at[e], own_sem.at[0])
    own_x.start()

    barrier = pltpu.get_barrier_semaphore()

    def greet_plane(s, carry):
        pl.semaphore_signal(barrier, inc=1, device_id=plane_peer(lax.rem(q + s, PLANE)), device_id_type=MESH)
        return carry

    def greet_z(s, carry):
        pl.semaphore_signal(barrier, inc=1, device_id=z_peer(lax.rem(z + s, DEPTH)), device_id_type=MESH)
        return carry

    lax.fori_loop(1, PLANE, greet_plane, 0)
    lax.fori_loop(1, DEPTH, greet_z, 0)
    pl.semaphore_signal(barrier, inc=1, device_id=mate, device_id_type=MESH)

    for load in loads[:4]:
        load.wait()
    cells = v_cell[...]
    cell_row = ((cells.astype(F32) + 0.5) * (1.0 / COLS)).astype(jnp.int32)
    cell_col = cells - cell_row * COLS
    tile = v_owner[...]
    value, a, b = v_innov[...], v_frac[0:1, :], v_frac[1:2, :]
    obs[0, 0:1, :] = ((tile >> 2) * ROWS + cell_row).astype(F32)
    obs[0, 1:2, :] = ((tile & 3) * COLS + cell_col).astype(F32)
    obs[0, 2:3, :] = value * (1.0 - a)
    obs[0, 3:4, :] = value * a
    obs[0, 4:5, :] = 1.0 - b
    obs[0, 5:6, :] = b
    obs[0, 6:8, :] = jnp.zeros((2, OBS), F32)

    first_col = (core * HALF).astype(F32)

    def spread(slot, start, first):
        at = pl.ds(start, CHUNK)
        row_table[...] = tent_table(obs[slot, 0:1, at], obs[slot, 2:3, at], obs[slot, 3:4, at], LAT)
        col_table[...] = tent_table(obs[slot, 1:2, at] - first_col, obs[slot, 4:5, at], obs[slot, 5:6, at], HALF)
        product = lax.dot_general(
            row_table[...], col_table[...], (((1,), (1,)), ((), ())), preferred_element_type=F32
        )
        if first:
            total[...] = product
        else:
            total[...] += product

    spread(0, 0, True)

    pl.semaphore_wait(barrier, PLANE - 1 + DEPTH - 1 + 1)
    obs_copy = remote(obs.at[0], obs.at[1], obs_sem.at[0], obs_sem.at[1], mate)
    obs_copy.start()

    def send_x(s, carry):
        to = lax.rem(e + s, 8)
        to_y, to_x = to // 4, lax.rem(to, 4)
        remote(
            anom.at[pl.ds(to_y * 8, 8), to_x], xrecv.at[e], x_sem.at[0], x_sem.at[1],
            {"lat": to_y * 8 + z, "lon": to_x},
        ).start()
        return carry

    lax.fori_loop(1, 8, send_x, 0)

    spread(0, CHUNK, False)
    obs_copy.wait_recv()
    spread(1, 0, False)
    spread(1, CHUNK, False)

    for p in range(PLANE):
        psend[p] = total[ROWS * p : ROWS * (p + 1), :].astype(BF16)

    def send_p(s, carry):
        to = lax.rem(q + s, PLANE)
        remote(psend.at[to], precv.at[q], p_sem.at[0], p_sem.at[1], plane_peer(to)).start()
        return carry

    lax.fori_loop(1, PLANE, send_p, 0)

    loads[4].wait()
    lat_t[...] = v_latk[...].astype(F32).T.astype(BF16)

    remote(
        psend.at[pl.ds(0, PLANE - 1)], precv.at[pl.ds(0, PLANE - 1)], p_sem.at[0], p_sem.at[1], mate
    ).wait_recv()
    band = total[pl.ds(pl.multiple_of(q * ROWS, 8), ROWS), :]
    for s in range(1, PLANE):
        band = band + precv[lax.rem(q + s, PLANE)].astype(F32)

    zsend[...] = band.astype(BF16)

    def send_z(s, carry):
        to = lax.rem(z + s, DEPTH)
        remote(zsend, zrecv.at[z], z_sem.at[0], z_sem.at[1], z_peer(to)).start()
        return carry

    lax.fori_loop(1, DEPTH, send_z, 0)

    remote(
        xrecv.at[pl.ds(0, 7)], xrecv.at[pl.ds(0, 7)], x_sem.at[0], x_sem.at[1], mate
    ).wait_recv()
    own_x.wait()
    for to in range(DEPTH):
        for y in range(2):
            fsend[to, ROWS * y : ROWS * (y + 1), :] = jnp.concatenate(
                [xrecv[y * 4 + x, to].astype(F32) for x in range(4)], axis=1
            ).astype(BF16)

    def send_f(s, carry):
        to = lax.rem(z + s, DEPTH)
        remote(fsend.at[to], frecv.at[z], f_sem.at[0], f_sem.at[1], z_peer(to)).start()
        return carry

    lax.fori_loop(1, DEPTH, send_f, 0)
    own_f = pltpu.make_async_copy(fsend.at[z], frecv.at[z], own_sem.at[1])
    own_f.start()

    remote(
        zrecv.at[pl.ds(0, DEPTH - 1)], zrecv.at[pl.ds(0, DEPTH - 1)], z_sem.at[0], z_sem.at[1], mate
    ).wait_recv()
    for s in range(1, DEPTH):
        band = band + zrecv[lax.rem(z + s, DEPTH)].astype(F32)
    forcing[core, q] = band.astype(BF16)

    def send_ag(s, carry):
        to = lax.rem(q + s, PLANE)
        remote(forcing.at[core, q], forcing.at[core, q], ag_send, ag_recv.at[q], plane_peer(to)).start()
        return carry

    lax.fori_loop(1, PLANE, send_ag, 0)

    def to_mate(p):
        return remote(forcing.at[core, p], forcing.at[core, p], core_sem.at[0], core_sem.at[1], mate)

    to_mate(q).start()

    def pass_on(s, carry):
        p = lax.rem(q + PLANE - s, PLANE)
        remote(forcing.at[core, p], forcing.at[core, p], ag_send, ag_recv.at[p], mate).wait_recv()
        to_mate(p).start()
        return carry

    lax.fori_loop(1, PLANE, pass_on, 0)

    remote(
        frecv.at[pl.ds(0, DEPTH - 1)], frecv.at[pl.ds(0, DEPTH - 1)], f_sem.at[0], f_sem.at[1], mate
    ).wait_recv()
    own_f.wait()
    loads[5].wait()
    remote(forcing.at[1 - core], forcing.at[1 - core], core_sem.at[0], core_sem.at[1], mate).wait_recv()

    for t in range(DEPTH):
        pair = []
        for band_at in (2 * t, 2 * t + 1):
            y, at = band_at // 8, band_at % 8
            field = frecv[at, ROWS * y : ROWS * (y + 1), :].astype(F32)
            factor = jnp.concatenate([forcing[0, band_at], forcing[1, band_at]], axis=1).astype(F32)
            pair.append(field * factor)
        weighted[2 * ROWS * t : 2 * ROWS * (t + 1), :] = jnp.concatenate(pair, axis=0).astype(BF16)

    low_lanes = lax.broadcasted_iota(jnp.int32, (8, 128), 1) < 64
    low_wide = lax.broadcasted_iota(jnp.int32, (ROWS, 128), 1) < 64

    for h in range(2):
        mixed = jnp.dot(lat_t[LAT // 2 * h : LAT // 2 * (h + 1), :], weighted[...], preferred_element_type=F32)
        grad = jnp.dot(mixed.astype(BF16), v_lonk[...], preferred_element_type=F32)
        for i in range(8):
            for pair_at in range(2):
                t0, t1, t2 = (
                    grad[ROWS * i : ROWS * (i + 1), 384 * pair_at + 128 * j : 384 * pair_at + 128 * (j + 1)]
                    for j in range(3)
                )
                r1, r2 = pltpu.roll(t1, 64, 1), pltpu.roll(t2, 64, 1)
                for odd, (main, low, high) in enumerate(
                    ((t0, t1, r1), (jnp.where(low_wide, r1, r2), r2, t2))
                ):
                    tail = jnp.where(low_lanes, low[0:8], high[8:16])
                    gsend[(8 * h + i) * 4 + 2 * pair_at + odd] = jnp.concatenate(
                        [main, tail, low[16:24]], axis=0
                    ).astype(BF16)

        def send_g(s, carry):
            to_lat = 8 * h + lax.rem(z + s // 4, 8)
            to_lon = lax.rem(lon + s, 4)
            to = to_lat * 4 + to_lon

            @pl.when(to != me)
            def _():
                remote(
                    gsend.at[to], grecv.at[me], g_send, g_recv.at[lat], {"lat": to_lat, "lon": to_lon}
                ).start()

            return carry

        lax.fori_loop(0, 32, send_g, 0)

    own_g = pltpu.make_async_copy(gsend.at[me], grecv.at[me], own_sem.at[2])
    own_g.start()
    own_g.wait()

    def take(s, carry):
        at = lax.rem(lat + s, 16)

        @pl.when(s == 0)
        def _():
            remote(grecv.at[pl.ds(0, 3)], grecv.at[pl.ds(0, 3)], g_send, g_recv.at[at], mate).wait_recv()

        @pl.when(s != 0)
        def _():
            remote(grecv.at[pl.ds(0, 4)], grecv.at[pl.ds(0, 4)], g_send, g_recv.at[at], mate).wait_recv()

        for k in range(LEVELS):
            block = grecv[at * 4 + k].astype(F32)
            tail = block[24:32]
            out_v[at, k, :, 0:128] = block[0:24].astype(BF16)
            out_v[at, k, :, 128:192] = jnp.concatenate(
                [tail, pltpu.roll(tail, 64, 1), block[32:40]], axis=0
            )[:, 0:64].astype(BF16)
        pltpu.make_async_copy(out_v.at[at], out.at[at], out_sem).start()
        return carry

    lax.fori_loop(0, 16, take, 0)
    pltpu.make_async_copy(out_v, out, out_sem).wait()

    obs_copy.wait_send()
    remote(xrecv.at[pl.ds(0, 7)], xrecv.at[pl.ds(0, 7)], x_sem.at[0], x_sem.at[1], mate).wait_send()
    remote(psend.at[pl.ds(0, 15)], psend.at[pl.ds(0, 15)], p_sem.at[0], p_sem.at[1], mate).wait_send()
    remote(zrecv.at[pl.ds(0, 7)], zrecv.at[pl.ds(0, 7)], z_sem.at[0], z_sem.at[1], mate).wait_send()
    remote(fsend.at[pl.ds(0, 7)], fsend.at[pl.ds(0, 7)], f_sem.at[0], f_sem.at[1], mate).wait_send()
    remote(psend.at[pl.ds(0, 15)], psend.at[pl.ds(0, 15)], ag_send, p_sem.at[1], mate).wait_send()
    remote(forcing.at[0], forcing.at[0], core_sem.at[0], core_sem.at[1], mate).wait_send()
    remote(gsend.at[pl.ds(0, 63)], gsend.at[pl.ds(0, 63)], g_send, p_sem.at[1], mate).wait_send()


def shards(anomalies, innovation, corner_frac, corner_cell, cell_owner, latitude_kernel, longitude_kernel):
    dma = pltpu.SemaphoreType.DMA
    return pl.pallas_call(
        kernel,
        out_shape=jax.ShapeDtypeStruct(anomalies.shape, BF16),
        in_specs=[pl.BlockSpec(memory_space=pl.ANY)] * 7,
        out_specs=pl.BlockSpec(memory_space=pl.ANY),
        scratch_shapes=[
            pltpu.VMEM((1, OBS), F32),
            pltpu.VMEM((2, OBS), F32),
            pltpu.VMEM((1, OBS), jnp.int32),
            pltpu.VMEM((1, OBS), jnp.int32),
            pltpu.VMEM((LAT, LAT), BF16),
            pltpu.VMEM((LON, LON), BF16),
            pltpu.VMEM((2, 8, OBS), F32),
            pltpu.VMEM((LAT, CHUNK), BF16),
            pltpu.VMEM((HALF, CHUNK), BF16),
            pltpu.VMEM((LAT, HALF), F32),
            pltpu.VMEM((PLANE, ROWS, HALF), BF16),
            pltpu.VMEM((PLANE, ROWS, HALF), BF16),
            pltpu.VMEM((ROWS, HALF), BF16),
            pltpu.VMEM((DEPTH, ROWS, HALF), BF16),
            pltpu.VMEM((2, PLANE, ROWS, HALF), BF16),
            pltpu.VMEM((8, 8, ROWS, COLS), BF16),
            pltpu.VMEM((DEPTH, 2 * ROWS, LON), BF16),
            pltpu.VMEM((DEPTH, 2 * ROWS, LON), BF16),
            pltpu.VMEM((LAT, LAT), BF16),
            pltpu.VMEM((LAT, LON), BF16),
            pltpu.VMEM((GROUP, PACKED, 128), BF16),
            pltpu.VMEM((GROUP, PACKED, 128), BF16),
            pltpu.VMEM((16, LEVELS, ROWS, COLS), BF16),
            dma((6,)),
            dma((3,)),
            dma,
            dma((2,)),
            dma((2,)),
            dma((2,)),
            dma((2,)),
            dma((2,)),
            dma,
            dma((PLANE,)),
            dma((2,)),
            dma,
            dma((16,)),
        ],
        compiler_params=pltpu.CompilerParams(
            collective_id=0, has_side_effects=True, vmem_limit_bytes=40 * 2**20
        ),
    )(
        anomalies,
        innovation.reshape(1, OBS),
        corner_frac,
        corner_cell.reshape(1, OBS),
        cell_owner.reshape(1, OBS),
        latitude_kernel,
        longitude_kernel,
    )


def solution(mesh):
    placed = (
        P("mem", None, "lat", "lon"),
        P(("mem", "lat", "lon")),
        P(None, ("mem", "lat", "lon")),
        P(("mem", "lat", "lon")),
        P(("mem", "lat", "lon")),
        P(),
        P(),
    )
    return jax.shard_map(
        shards, mesh=mesh, in_specs=placed, out_specs=P("mem", None, "lat", "lon"), check_vma=False
    )
```

```python
import functools

import jax
import jax.numpy as jnp
from jax import lax
from jax.experimental import pallas as pl
from jax.experimental.pallas import tpu as pltpu
from jax.sharding import PartitionSpec as P

MESH = pl.DeviceIdType.MESH
F32 = jnp.float32
BF16 = jnp.bfloat16

LEVELS, ROWS, COLS = 4, 24, 192
LAT, LON, OBS = 384, 768, 4096
HALF = LON // 2
PLANE, DEPTH, GROUP = 16, 8, 64
CHUNK = 2048
PACKED = 36


def tent_table(index, low, high, count):
    width = index.shape[1]
    low, high = low.astype(BF16), high.astype(BF16)
    rows = lax.broadcasted_iota(jnp.int32, (128, width), 0).astype(F32).astype(BF16)
    parts = []
    for base in range(0, count, 128):
        at = (index - base).astype(BF16)
        after = (index - (base - 1)).astype(BF16)
        parts.append(jnp.where(rows == at, low, jnp.where(rows == after, high, BF16(0))))
    return jnp.concatenate(parts, axis=0)


def unpack(packed):
    eight, four = packed[24:32], packed[32:36]
    tail = jnp.concatenate([eight[:, 0:64], eight[:, 64:128], four[:, 0:64], four[:, 64:128]], axis=0)
    return jnp.concatenate([packed[0:24], tail], axis=1)


def kernel(
    anom, innov, frac, cell, owner, lat_k, lon_k, out,
    v_innov, v_frac, v_cell, v_owner, v_latk, v_lonk,
    obs, row_table, col_table, total,
    psend, precv, zsend, zrecv, forcing,
    v_anom, fsend, frecv, field, lat_t, weighted, gsend, grecv,
    load_sem, own_sem,
    obs_sem, p_sem, z_sem, f_sem, x_sem, ag_sem, core_sem, g_send, g_recv,
):
    mem, lat, lon = lax.axis_index("mem"), lax.axis_index("lat"), lax.axis_index("lon")
    core, y_lo = lax.rem(mem, 2), mem // 2
    z, y_hi = lax.rem(lat, 8), lat // 8
    q = (y_hi * 2 + y_lo) * 4 + lon
    e = y_hi * 4 + lon
    me = lat * 4 + lon
    mate = {"mem": mem + 1 - 2 * core}

    def plane_peer(p):
        y = p // 4
        return {"mem": lax.rem(y, 2) * 2 + core, "lat": (y // 2) * 8 + z, "lon": lax.rem(p, 4)}

    def z_peer(to):
        return {"lat": y_hi * 8 + to}

    def remote(src, dst, send, recv, to):
        return pltpu.make_async_remote_copy(
            src_ref=src, dst_ref=dst, send_sem=send, recv_sem=recv, device_id=to, device_id_type=MESH
        )

    owed, sent = {}, []

    def expect(name, block, count, sems, start=0):
        some = block.at[pl.ds(0, count)]
        owed[name] = remote(some, some, sems.at[0], sems.at[1], mate).wait_recv
        sent.append(remote(some, some, sems.at[0], sems.at[1], mate).wait_send)

    loads = [
        pltpu.make_async_copy(src, dst, load_sem.at[i])
        for i, (src, dst) in enumerate(
            ((innov, v_innov), (frac, v_frac), (cell, v_cell), (owner, v_owner), (anom, v_anom), (lat_k, v_latk), (lon_k, v_lonk))
        )
    ]
    for i, load in enumerate(loads):
        load.start()
        owed[i] = load.wait

    barrier = pltpu.get_barrier_semaphore()

    def greet_plane(s, carry):
        pl.semaphore_signal(barrier, inc=1, device_id=plane_peer(lax.rem(q + s, PLANE)), device_id_type=MESH)
        return carry

    def greet_z(s, carry):
        pl.semaphore_signal(barrier, inc=1, device_id=z_peer(lax.rem(z + s, DEPTH)), device_id_type=MESH)
        return carry

    lax.fori_loop(1, PLANE, greet_plane, 0)
    lax.fori_loop(1, DEPTH, greet_z, 0)
    pl.semaphore_signal(barrier, inc=1, device_id=mate, device_id_type=MESH)

    for i in range(4):
        owed.pop(i)()
    cells = v_cell[...]
    cell_row = ((cells.astype(F32) + 0.5) * (1.0 / COLS)).astype(jnp.int32)
    cell_col = cells - cell_row * COLS
    tile = v_owner[...]
    value, a, b = v_innov[...], v_frac[0:1, :], v_frac[1:2, :]
    obs[0, 0:1, :] = ((tile >> 2) * ROWS + cell_row).astype(F32)
    obs[0, 1:2, :] = ((tile & 3) * COLS + cell_col).astype(F32)
    obs[0, 2:3, :] = value * (1.0 - a)
    obs[0, 3:4, :] = value * a
    obs[0, 4:5, :] = 1.0 - b
    obs[0, 5:6, :] = b
    obs[0, 6:8, :] = jnp.zeros((2, OBS), F32)

    first_col = (core * HALF).astype(F32)

    def tables(slot, start):
        at, use = pl.ds(start, CHUNK), (2 * slot + start // CHUNK) % 2
        row_table[use] = tent_table(obs[slot, 0:1, at], obs[slot, 2:3, at], obs[slot, 3:4, at], LAT)
        col_table[use] = tent_table(obs[slot, 1:2, at] - first_col, obs[slot, 4:5, at], obs[slot, 5:6, at], HALF)

    def spread(part):
        product = lax.dot_general(
            row_table[part % 2], col_table[part % 2], (((1,), (1,)), ((), ())), preferred_element_type=F32
        )
        if part == 0:
            total[...] = product
        else:
            total[...] += product

    tables(0, 0)

    owed.pop(4)()

    def pack(m, carry):
        for k in range(LEVELS):
            block = v_anom[m, k].astype(F32)
            tail = block[:, 128:192]
            fsend[lax.rem(m, 8), m // 8, k] = jnp.concatenate(
                [
                    block[:, 0:128],
                    jnp.concatenate([tail[0:8], tail[8:16]], axis=1),
                    jnp.concatenate([tail[16:20], tail[20:24]], axis=1),
                ],
                axis=0,
            ).astype(BF16)
        return carry

    lax.fori_loop(0, 16, pack, 0, unroll=2)

    pl.semaphore_wait(barrier, PLANE - 1 + DEPTH - 1 + 1)
    obs_copy = remote(obs.at[0], obs.at[1], obs_sem.at[0], obs_sem.at[1], mate)
    obs_copy.start()
    owed["obs"] = obs_copy.wait_recv
    sent.append(obs_copy.wait_send)

    offs = (4, 3, -3, 2, -2, 1, -1)

    def first_leg(leg, slots):
        for i in slots:
            to = lax.rem(z - offs[i - 1] + DEPTH, DEPTH)
            remote(fsend.at[to], frecv.at[i], f_sem.at[leg, 0], f_sem.at[leg, 1], z_peer(to)).start()
        expect("f%d" % leg, fsend, len(slots), f_sem.at[leg])

    first_leg(0, (1, 2, 3))
    own_f = pltpu.make_async_copy(fsend.at[z], frecv.at[0], own_sem.at[0])
    own_f.start()
    owed["own_f"] = own_f.wait

    spread(0)
    tables(0, CHUNK)
    owed.pop("obs")()
    spread(1)
    tables(1, 0)
    spread(2)
    tables(1, CHUNK)
    spread(3)

    for p in range(PLANE):
        psend[p] = total[ROWS * p : ROWS * (p + 1), :].astype(BF16)

    def send_p(s, carry):
        to = lax.rem(q + s, PLANE)
        remote(psend.at[to], precv.at[q], p_sem.at[0], p_sem.at[1], plane_peer(to)).start()
        return carry

    lax.fori_loop(1, PLANE, send_p, 0)
    expect("p", psend, PLANE - 1, p_sem)

    owed.pop(5)()
    lat_t[...] = v_latk[...].astype(F32).T.astype(BF16)

    owed.pop("p")()
    band = total[pl.ds(pl.multiple_of(q * ROWS, 8), ROWS), :]
    for s in range(1, PLANE):
        band = band + precv[lax.rem(q + s, PLANE)].astype(F32)

    zsend[...] = band.astype(BF16)

    def send_z(s, carry):
        to = lax.rem(z + s, DEPTH)
        remote(zsend, zrecv.at[z], z_sem.at[0], z_sem.at[1], z_peer(to)).start()
        return carry

    lax.fori_loop(1, DEPTH, send_z, 0)
    expect("z", zrecv, DEPTH - 1, z_sem)
    first_leg(1, (4, 5, 6, 7))

    def second_leg(half):
        slots = pl.ds(4 * half, 4)
        for i in range(1, 8):
            to = lax.rem(e + i, 8)
            to_y, to_x = to // 4, lax.rem(to, 4)
            remote(
                frecv.at[slots, to_y, to_x], field.at[e, slots], x_sem.at[half, 0], x_sem.at[half, 1],
                {"lat": to_y * 8 + z, "lon": to_x},
            ).start()
        some = field.at[pl.ds(0, 7), pl.ds(0, 4)]
        copy = remote(some, some, x_sem.at[half, 0], x_sem.at[half, 1], mate)
        owed["x%d" % half] = copy.wait_recv
        sent.append(copy.wait_send)

    owed.pop("f0")()
    owed.pop("own_f")()
    second_leg(0)

    owed.pop("z")()
    for s in range(1, DEPTH):
        band = band + zrecv[lax.rem(z + s, DEPTH)].astype(F32)
    forcing[core, q] = band.astype(BF16)

    def send_ag(s, carry):
        to = lax.rem(q + s, PLANE)
        remote(forcing.at[core, q], forcing.at[core, q], ag_sem.at[0], ag_sem.at[1], plane_peer(to)).start()
        return carry

    lax.fori_loop(1, PLANE, send_ag, 0)
    expect("ag", psend, PLANE - 1, ag_sem)
    owed.pop("f1")()
    second_leg(1)
    own_x = pltpu.make_async_copy(frecv.at[:, y_hi, lon], field.at[e], own_sem.at[1])
    own_x.start()
    owed["own_x"] = own_x.wait
    owed.pop("ag")()
    halves = remote(forcing.at[core], forcing.at[core], core_sem.at[0], core_sem.at[1], mate)
    halves.start()
    owed["half"] = halves.wait_recv
    sent.append(halves.wait_send)

    owed.pop("half")()
    owed.pop("x0")()
    owed.pop("x1")()
    owed.pop("own_x")()
    owed.pop(6)()

    for t in range(DEPTH):
        pair = []
        for band_at in (2 * t, 2 * t + 1):
            y, ahead = band_at // 8, lax.rem(band_at % 8 - z + DEPTH, DEPTH)
            slot = lax.rem(jnp.maximum(2 * ahead - 7, 8 - 2 * ahead), DEPTH)
            row = jnp.concatenate([unpack(field[y * 4 + x, slot].astype(F32)) for x in range(4)], axis=1)
            factor = jnp.concatenate([forcing[0, band_at], forcing[1, band_at]], axis=1).astype(F32)
            pair.append(row * factor)
        weighted[2 * ROWS * t : 2 * ROWS * (t + 1), :] = jnp.concatenate(pair, axis=0).astype(BF16)

    low_lanes = lax.broadcasted_iota(jnp.int32, (8, 128), 1) < 64
    low_wide = lax.broadcasted_iota(jnp.int32, (ROWS, 128), 1) < 64

    for h in range(2):
        mixed = jnp.dot(lat_t[LAT // 2 * h : LAT // 2 * (h + 1), :], weighted[...], preferred_element_type=F32)
        high = mixed.astype(BF16)
        both = jnp.concatenate([high, (mixed - high.astype(F32)).astype(BF16)], axis=0)
        both = jnp.dot(both, v_lonk[...], preferred_element_type=F32)
        grad = both[: LAT // 2] + both[LAT // 2 :]
        for i in range(8):
            for pair_at in range(2):
                t0, t1, t2 = (
                    grad[ROWS * i : ROWS * (i + 1), 384 * pair_at + 128 * j : 384 * pair_at + 128 * (j + 1)]
                    for j in range(3)
                )
                r1, r2 = pltpu.roll(t1, 64, 1), pltpu.roll(t2, 64, 1)
                for odd, (main, low, high) in enumerate(
                    ((t0, t1, r1), (jnp.where(low_wide, r1, r2), r2, t2))
                ):
                    eight = jnp.where(low_lanes, low[0:8], high[8:16])
                    four = jnp.where(low_lanes, low[16:24], pltpu.roll(high[16:24], 4, 0))
                    gsend[(8 * h + i) * 4 + 2 * pair_at + odd] = jnp.concatenate(
                        [main, eight, four[0:4]], axis=0
                    ).astype(BF16)

        def send_g(s, carry):
            to_lat = 8 * h + lax.rem(z + s // 4, 8)
            to_lon = lax.rem(lon + s, 4)
            to = to_lat * 4 + to_lon

            @pl.when(to != me)
            def _():
                remote(
                    gsend.at[to], grecv.at[me], g_send, g_recv.at[lat], {"lat": to_lat, "lon": to_lon}
                ).start()

            return carry

        lax.fori_loop(0, 32, send_g, 0)

    own_g = pltpu.make_async_copy(gsend.at[me], grecv.at[me], own_sem.at[2])
    own_g.start()
    own_g.wait()

    def take(s, carry):
        at = lax.rem(lat + s, 16)

        @pl.when(s == 0)
        def _():
            remote(grecv.at[pl.ds(0, 3)], grecv.at[pl.ds(0, 3)], g_send, g_recv.at[at], mate).wait_recv()

        @pl.when(s != 0)
        def _():
            remote(grecv.at[pl.ds(0, 4)], grecv.at[pl.ds(0, 4)], g_send, g_recv.at[at], mate).wait_recv()

        for k in range(LEVELS):
            out[at, k] = unpack(grecv[at * 4 + k].astype(F32)).astype(BF16)
        return carry

    lax.fori_loop(0, 16, take, 0)

    some = gsend.at[pl.ds(0, GROUP - 1)]
    remote(some, some, g_send, p_sem.at[1], mate).wait_send()
    for wait in sent:
        wait()


def shards(anomalies, innovation, corner_frac, corner_cell, cell_owner, latitude_kernel, longitude_kernel):
    dma = pltpu.SemaphoreType.DMA
    return pl.pallas_call(
        kernel,
        out_shape=pltpu.VMEM(anomalies.shape, BF16),
        in_specs=[pl.BlockSpec(memory_space=pltpu.HBM)] * 7,
        out_specs=pl.BlockSpec(memory_space=pltpu.VMEM),
        scratch_shapes=[
            pltpu.VMEM((1, OBS), F32),
            pltpu.VMEM((2, OBS), F32),
            pltpu.VMEM((1, OBS), jnp.int32),
            pltpu.VMEM((1, OBS), jnp.int32),
            pltpu.VMEM((LAT, LAT), BF16),
            pltpu.VMEM((LON, LON), BF16),
            pltpu.VMEM((2, 8, OBS), F32),
            pltpu.VMEM((2, LAT, CHUNK), BF16),
            pltpu.VMEM((2, HALF, CHUNK), BF16),
            pltpu.VMEM((LAT, HALF), F32),
            pltpu.VMEM((PLANE, ROWS, HALF), BF16),
            pltpu.VMEM((PLANE, ROWS, HALF), BF16),
            pltpu.VMEM((ROWS, HALF), BF16),
            pltpu.VMEM((DEPTH, ROWS, HALF), BF16),
            pltpu.VMEM((2, PLANE, ROWS, HALF), BF16),
            pltpu.VMEM((16, LEVELS, ROWS, COLS), BF16),
            pltpu.VMEM((DEPTH, 2, LEVELS, PACKED, 128), BF16),
            pltpu.VMEM((DEPTH, 2, LEVELS, PACKED, 128), BF16),
            pltpu.VMEM((8, DEPTH, PACKED, 128), BF16),
            pltpu.VMEM((LAT, LAT), BF16),
            pltpu.VMEM((LAT, LON), BF16),
            pltpu.VMEM((GROUP, PACKED, 128), BF16),
            pltpu.VMEM((GROUP, PACKED, 128), BF16),
            dma((7,)),
            dma((3,)),
            dma((2,)),
            dma((2,)),
            dma((2,)),
            dma((2, 2)),
            dma((2, 2)),
            dma((2,)),
            dma((2,)),
            dma,
            dma((16,)),
        ],
        compiler_params=pltpu.CompilerParams(
            collective_id=0, has_side_effects=True, vmem_limit_bytes=60 * 2**20
        ),
    )(*(
        pltpu.with_memory_space_constraint(x, pltpu.HBM)
        for x in (
            anomalies,
            innovation.reshape(1, OBS),
            corner_frac,
            corner_cell.reshape(1, OBS),
            cell_owner.reshape(1, OBS),
            latitude_kernel,
            longitude_kernel,
        )
    ))


def solution(mesh):
    placed = (
        P("mem", None, "lat", "lon"),
        P(("mem", "lat", "lon")),
        P(None, ("mem", "lat", "lon")),
        P(("mem", "lat", "lon")),
        P(("mem", "lat", "lon")),
        P(),
        P(),
    )
    return jax.shard_map(
        shards, mesh=mesh, in_specs=placed, out_specs=P("mem", None, "lat", "lon"), check_vma=False
    )
```

```python
import functools

import jax
import jax.numpy as jnp
from jax import lax
from jax.experimental import pallas as pl
from jax.experimental.pallas import tpu as pltpu
from jax.sharding import PartitionSpec as P

MESH = pl.DeviceIdType.MESH
F32 = jnp.float32
BF16 = jnp.bfloat16

LEVELS, ROWS, COLS = 4, 24, 192
LAT, LON, OBS = 384, 768, 4096
HALF = LON // 2
PLANE, DEPTH, GROUP = 16, 8, 64
CHUNK = 2048
PACKED = 36


def tent_table(index, low, high, count):
    width = index.shape[1]
    low, high = low.astype(BF16), high.astype(BF16)
    rows = lax.broadcasted_iota(jnp.int32, (128, width), 0).astype(F32).astype(BF16)
    parts = []
    for base in range(0, count, 128):
        at = (index - base).astype(BF16)
        after = (index - (base - 1)).astype(BF16)
        parts.append(jnp.where(rows == at, low, jnp.where(rows == after, high, BF16(0))))
    return jnp.concatenate(parts, axis=0)


def unpack(packed):
    eight, four = packed[24:32], packed[32:36]
    tail = jnp.concatenate([eight[:, 0:64], eight[:, 64:128], four[:, 0:64], four[:, 64:128]], axis=0)
    return jnp.concatenate([packed[0:24], tail], axis=1)


def kernel(
    anom, innov, frac, cell, owner, lat_k, lon_k, out,
    v_innov, v_frac, v_cell, v_owner, v_latk, v_lonk,
    obs, row_table, col_table, total, hsend, hrecv,
    psend, precv, zsend, zrecv, forcing,
    v_anom, fsend, frecv, field, lat_t, weighted, gsend, grecv,
    load_sem, own_sem,
    h_sem, p_sem, z_sem, f_sem, x_sem, ag_sem, core_sem, g_send, g_recv,
):
    mem, lat, lon = lax.axis_index("mem"), lax.axis_index("lat"), lax.axis_index("lon")
    core, y_lo = lax.rem(mem, 2), mem // 2
    z, y_hi = lax.rem(lat, 8), lat // 8
    q = (y_hi * 2 + y_lo) * 4 + lon
    e = y_hi * 4 + lon
    me = lat * 4 + lon
    mate = {"mem": mem + 1 - 2 * core}

    def plane_peer(p):
        y = p // 4
        return {"mem": lax.rem(y, 2) * 2 + core, "lat": (y // 2) * 8 + z, "lon": lax.rem(p, 4)}

    def z_peer(to):
        return {"lat": y_hi * 8 + to}

    def remote(src, dst, send, recv, to):
        return pltpu.make_async_remote_copy(
            src_ref=src, dst_ref=dst, send_sem=send, recv_sem=recv, device_id=to, device_id_type=MESH
        )

    owed, sent = {}, []

    def expect(name, block, count, sems, start=0):
        some = block.at[pl.ds(0, count)]
        owed[name] = remote(some, some, sems.at[0], sems.at[1], mate).wait_recv
        sent.append(remote(some, some, sems.at[0], sems.at[1], mate).wait_send)

    loads = [
        pltpu.make_async_copy(src, dst, load_sem.at[i])
        for i, (src, dst) in enumerate(
            ((innov, v_innov), (frac, v_frac), (cell, v_cell), (owner, v_owner), (anom, v_anom), (lat_k, v_latk), (lon_k, v_lonk))
        )
    ]
    for i, load in enumerate(loads):
        load.start()
        owed[i] = load.wait

    barrier = pltpu.get_barrier_semaphore()

    def greet_plane(s, carry):
        pl.semaphore_signal(barrier, inc=1, device_id=plane_peer(lax.rem(q + s, PLANE)), device_id_type=MESH)
        return carry

    def greet_z(s, carry):
        pl.semaphore_signal(barrier, inc=1, device_id=z_peer(lax.rem(z + s, DEPTH)), device_id_type=MESH)
        return carry

    lax.fori_loop(1, PLANE, greet_plane, 0)
    lax.fori_loop(1, DEPTH, greet_z, 0)
    pl.semaphore_signal(barrier, inc=1, device_id=mate, device_id_type=MESH)

    for i in range(4):
        owed.pop(i)()
    cells = v_cell[...]
    cell_row = ((cells.astype(F32) + 0.5) * (1.0 / COLS)).astype(jnp.int32)
    cell_col = cells - cell_row * COLS
    tile = v_owner[...]
    value, a, b = v_innov[...], v_frac[0:1, :], v_frac[1:2, :]
    obs[0:1, :] = ((tile >> 2) * ROWS + cell_row).astype(F32)
    obs[1:2, :] = ((tile & 3) * COLS + cell_col).astype(F32)
    obs[2:3, :] = value * (1.0 - a)
    obs[3:4, :] = value * a
    obs[4:5, :] = 1.0 - b
    obs[5:6, :] = b

    def rows_of(part):
        at = pl.ds(part * CHUNK, CHUNK)
        row_table[part] = tent_table(obs[0:1, at], obs[2:3, at], obs[3:4, at], LAT)

    def cols_of(part, half, use):
        at, first = pl.ds(part * CHUNK, CHUNK), (half * HALF).astype(F32)
        col_table[use] = tent_table(obs[1:2, at] - first, obs[4:5, at], obs[5:6, at], HALF)

    def spread(part, use):
        return lax.dot_general(
            row_table[part], col_table[use], (((1,), (1,)), ((), ())), preferred_element_type=F32
        )

    owed.pop(4)()

    def pack(m, carry):
        for k in range(LEVELS):
            block = v_anom[m, k].astype(F32)
            tail = block[:, 128:192]
            fsend[lax.rem(m, 8), m // 8, k] = jnp.concatenate(
                [
                    block[:, 0:128],
                    jnp.concatenate([tail[0:8], tail[8:16]], axis=1),
                    jnp.concatenate([tail[16:20], tail[20:24]], axis=1),
                ],
                axis=0,
            ).astype(BF16)
        return carry

    lax.fori_loop(0, 16, pack, 0, unroll=2)

    rows_of(0)
    cols_of(0, 1 - core, 0)
    total[...] = spread(0, 0)
    rows_of(1)
    cols_of(1, 1 - core, 1)
    total[...] += spread(1, 1)
    for p in range(PLANE):
        hsend[p] = total[ROWS * p : ROWS * (p + 1), :].astype(BF16)

    pl.semaphore_wait(barrier, PLANE - 1 + DEPTH - 1 + 1)
    swap = remote(hsend, hrecv, h_sem.at[0], h_sem.at[1], mate)
    swap.start()
    owed["swap"] = swap.wait_recv
    sent.append(swap.wait_send)

    offs = (4, 3, -3, 2, -2, 1, -1)

    def first_leg(leg, slots):
        for i in slots:
            to = lax.rem(z - offs[i - 1] + DEPTH, DEPTH)
            remote(fsend.at[to], frecv.at[i], f_sem.at[leg, 0], f_sem.at[leg, 1], z_peer(to)).start()
        expect("f%d" % leg, fsend, len(slots), f_sem.at[leg])

    first_leg(0, (1, 2, 3))
    own_f = pltpu.make_async_copy(fsend.at[z], frecv.at[0], own_sem.at[0])
    own_f.start()
    owed["own_f"] = own_f.wait

    cols_of(0, core, 2)
    total[...] = spread(0, 2)
    cols_of(1, core, 3)
    total[...] += spread(1, 3)
    owed.pop("swap")()

    for p in range(PLANE):
        psend[p] = (total[ROWS * p : ROWS * (p + 1), :] + hrecv[p].astype(F32)).astype(BF16)

    def send_p(s, carry):
        to = lax.rem(q + s, PLANE)
        remote(psend.at[to], precv.at[q], p_sem.at[0], p_sem.at[1], plane_peer(to)).start()
        return carry

    lax.fori_loop(1, PLANE, send_p, 0)
    expect("p", psend, PLANE - 1, p_sem)

    owed.pop(5)()
    lat_t[...] = v_latk[...].astype(F32).T.astype(BF16)

    owed.pop("p")()
    band = total[pl.ds(pl.multiple_of(q * ROWS, 8), ROWS), :] + hrecv[q].astype(F32)
    for s in range(1, PLANE):
        band = band + precv[lax.rem(q + s, PLANE)].astype(F32)

    zsend[...] = band.astype(BF16)

    def send_z(s, carry):
        to = lax.rem(z + s, DEPTH)
        remote(zsend, zrecv.at[z], z_sem.at[0], z_sem.at[1], z_peer(to)).start()
        return carry

    lax.fori_loop(1, DEPTH, send_z, 0)
    expect("z", zrecv, DEPTH - 1, z_sem)
    first_leg(1, (4, 5, 6, 7))

    def second_leg(half):
        slots = pl.ds(4 * half, 4)
        for i in range(1, 8):
            to = lax.rem(e + i, 8)
            to_y, to_x = to // 4, lax.rem(to, 4)
            remote(
                frecv.at[slots, to_y, to_x], field.at[e, slots], x_sem.at[half, 0], x_sem.at[half, 1],
                {"lat": to_y * 8 + z, "lon": to_x},
            ).start()
        some = field.at[pl.ds(0, 7), pl.ds(0, 4)]
        copy = remote(some, some, x_sem.at[half, 0], x_sem.at[half, 1], mate)
        owed["x%d" % half] = copy.wait_recv
        sent.append(copy.wait_send)

    owed.pop("f0")()
    owed.pop("own_f")()
    second_leg(0)

    owed.pop("z")()
    for s in range(1, DEPTH):
        band = band + zrecv[lax.rem(z + s, DEPTH)].astype(F32)
    forcing[core, q] = band.astype(BF16)

    def send_ag(s, carry):
        to = lax.rem(q + s, PLANE)
        remote(forcing.at[core, q], forcing.at[core, q], ag_sem.at[0], ag_sem.at[1], plane_peer(to)).start()
        return carry

    lax.fori_loop(1, PLANE, send_ag, 0)
    expect("ag", psend, PLANE - 1, ag_sem)
    owed.pop("f1")()
    second_leg(1)
    own_x = pltpu.make_async_copy(frecv.at[:, y_hi, lon], field.at[e], own_sem.at[1])
    own_x.start()
    owed["own_x"] = own_x.wait
    owed.pop("ag")()
    halves = remote(forcing.at[core], forcing.at[core], core_sem.at[0], core_sem.at[1], mate)
    halves.start()
    owed["half"] = halves.wait_recv
    sent.append(halves.wait_send)

    owed.pop("half")()
    owed.pop("x0")()
    owed.pop("x1")()
    owed.pop("own_x")()
    owed.pop(6)()

    for t in range(DEPTH):
        pair = []
        for band_at in (2 * t, 2 * t + 1):
            y, ahead = band_at // 8, lax.rem(band_at % 8 - z + DEPTH, DEPTH)
            slot = lax.rem(jnp.maximum(2 * ahead - 7, 8 - 2 * ahead), DEPTH)
            row = jnp.concatenate([unpack(field[y * 4 + x, slot].astype(F32)) for x in range(4)], axis=1)
            factor = jnp.concatenate([forcing[0, band_at], forcing[1, band_at]], axis=1).astype(F32)
            pair.append(row * factor)
        weighted[2 * ROWS * t : 2 * ROWS * (t + 1), :] = jnp.concatenate(pair, axis=0).astype(BF16)

    low_lanes = lax.broadcasted_iota(jnp.int32, (8, 128), 1) < 64
    low_wide = lax.broadcasted_iota(jnp.int32, (ROWS, 128), 1) < 64

    for h in range(4):
        mixed = jnp.dot(lat_t[LAT // 4 * h : LAT // 4 * (h + 1), :], weighted[...], preferred_element_type=F32)
        high = mixed.astype(BF16)
        both = jnp.concatenate([high, (mixed - high.astype(F32)).astype(BF16)], axis=0)
        both = jnp.dot(both, v_lonk[...], preferred_element_type=F32)
        grad = both[: LAT // 4] + both[LAT // 4 :]
        for i in range(4):
            for pair_at in range(2):
                t0, t1, t2 = (
                    grad[ROWS * i : ROWS * (i + 1), 384 * pair_at + 128 * j : 384 * pair_at + 128 * (j + 1)]
                    for j in range(3)
                )
                r1, r2 = pltpu.roll(t1, 64, 1), pltpu.roll(t2, 64, 1)
                for odd, (main, low, high) in enumerate(
                    ((t0, t1, r1), (jnp.where(low_wide, r1, r2), r2, t2))
                ):
                    eight = jnp.where(low_lanes, low[0:8], high[8:16])
                    four = jnp.where(low_lanes, low[16:24], pltpu.roll(high[16:24], 4, 0))
                    gsend[(4 * h + i) * 4 + 2 * pair_at + odd] = jnp.concatenate(
                        [main, eight, four[0:4]], axis=0
                    ).astype(BF16)

        def send_g(s, carry):
            to_lat = 4 * h + lax.rem(z + s // 4, 4)
            to_lon = lax.rem(lon + s, 4)
            to = to_lat * 4 + to_lon

            @pl.when(to != me)
            def _():
                remote(
                    gsend.at[to], grecv.at[me], g_send, g_recv.at[lat], {"lat": to_lat, "lon": to_lon}
                ).start()

            return carry

        lax.fori_loop(0, 16, send_g, 0)

    own_g = pltpu.make_async_copy(gsend.at[me], grecv.at[me], own_sem.at[2])
    own_g.start()
    own_g.wait()

    def take(s, carry):
        at = lax.rem(lat + s, 16)

        @pl.when(s == 0)
        def _():
            remote(grecv.at[pl.ds(0, 3)], grecv.at[pl.ds(0, 3)], g_send, g_recv.at[at], mate).wait_recv()

        @pl.when(s != 0)
        def _():
            remote(grecv.at[pl.ds(0, 4)], grecv.at[pl.ds(0, 4)], g_send, g_recv.at[at], mate).wait_recv()

        for k in range(LEVELS):
            out[at, k] = unpack(grecv[at * 4 + k].astype(F32)).astype(BF16)
        return carry

    lax.fori_loop(0, 16, take, 0)

    some = gsend.at[pl.ds(0, GROUP - 1)]
    remote(some, some, g_send, p_sem.at[1], mate).wait_send()
    for wait in sent:
        wait()


def shards(anomalies, innovation, corner_frac, corner_cell, cell_owner, latitude_kernel, longitude_kernel):
    dma = pltpu.SemaphoreType.DMA
    return pl.pallas_call(
        kernel,
        out_shape=pltpu.VMEM(anomalies.shape, BF16),
        in_specs=[pl.BlockSpec(memory_space=pltpu.HBM)] * 7,
        out_specs=pl.BlockSpec(memory_space=pltpu.VMEM),
        scratch_shapes=[
            pltpu.VMEM((1, OBS), F32),
            pltpu.VMEM((2, OBS), F32),
            pltpu.VMEM((1, OBS), jnp.int32),
            pltpu.VMEM((1, OBS), jnp.int32),
            pltpu.VMEM((LAT, LAT), BF16),
            pltpu.VMEM((LON, LON), BF16),
            pltpu.VMEM((8, OBS), F32),
            pltpu.VMEM((2, LAT, CHUNK), BF16),
            pltpu.VMEM((4, HALF, CHUNK), BF16),
            pltpu.VMEM((LAT, HALF), F32),
            pltpu.VMEM((PLANE, ROWS, HALF), BF16),
            pltpu.VMEM((PLANE, ROWS, HALF), BF16),
            pltpu.VMEM((PLANE, ROWS, HALF), BF16),
            pltpu.VMEM((PLANE, ROWS, HALF), BF16),
            pltpu.VMEM((ROWS, HALF), BF16),
            pltpu.VMEM((DEPTH, ROWS, HALF), BF16),
            pltpu.VMEM((2, PLANE, ROWS, HALF), BF16),
            pltpu.VMEM((16, LEVELS, ROWS, COLS), BF16),
            pltpu.VMEM((DEPTH, 2, LEVELS, PACKED, 128), BF16),
            pltpu.VMEM((DEPTH, 2, LEVELS, PACKED, 128), BF16),
            pltpu.VMEM((8, DEPTH, PACKED, 128), BF16),
            pltpu.VMEM((LAT, LAT), BF16),
            pltpu.VMEM((LAT, LON), BF16),
            pltpu.VMEM((GROUP, PACKED, 128), BF16),
            pltpu.VMEM((GROUP, PACKED, 128), BF16),
            dma((7,)),
            dma((3,)),
            dma((2,)),
            dma((2,)),
            dma((2,)),
            dma((2, 2)),
            dma((2, 2)),
            dma((2,)),
            dma((2,)),
            dma,
            dma((16,)),
        ],
        compiler_params=pltpu.CompilerParams(
            collective_id=0, has_side_effects=True, vmem_limit_bytes=60 * 2**20
        ),
    )(*(
        pltpu.with_memory_space_constraint(x, pltpu.HBM)
        for x in (
            anomalies,
            innovation.reshape(1, OBS),
            corner_frac,
            corner_cell.reshape(1, OBS),
            cell_owner.reshape(1, OBS),
            latitude_kernel,
            longitude_kernel,
        )
    ))


def solution(mesh):
    placed = (
        P("mem", None, "lat", "lon"),
        P(("mem", "lat", "lon")),
        P(None, ("mem", "lat", "lon")),
        P(("mem", "lat", "lon")),
        P(("mem", "lat", "lon")),
        P(),
        P(),
    )
    return jax.shard_map(
        shards, mesh=mesh, in_specs=placed, out_specs=P("mem", None, "lat", "lon"), check_vma=False
    )
```

```python
import functools

import jax
import jax.numpy as jnp
from jax import lax
from jax.experimental import pallas as pl
from jax.experimental.pallas import tpu as pltpu
from jax.sharding import PartitionSpec as P

MESH = pl.DeviceIdType.MESH
F32 = jnp.float32
BF16 = jnp.bfloat16

LEVELS, ROWS, COLS = 4, 24, 192
LAT, LON, OBS = 384, 768, 4096
HALF = LON // 2
PLANE, DEPTH, GROUP = 16, 8, 64
CHUNK = 4096
PACKED = 36


def tent_table(index, low, high, count):
    width = index.shape[1]
    low, high = low.astype(BF16), high.astype(BF16)
    rows = lax.broadcasted_iota(jnp.int32, (128, width), 0).astype(F32).astype(BF16)
    parts = []
    for base in range(0, count, 128):
        at = (index - base).astype(BF16)
        after = (index - (base - 1)).astype(BF16)
        parts.append(jnp.where(rows == at, low, jnp.where(rows == after, high, BF16(0))))
    return jnp.concatenate(parts, axis=0)


def unpack(packed):
    eight, four = packed[24:32], packed[32:36]
    tail = jnp.concatenate([eight[:, 0:64], eight[:, 64:128], four[:, 0:64], four[:, 64:128]], axis=0)
    return jnp.concatenate([packed[0:24], tail], axis=1)


def kernel(
    anom, innov, frac, cell, owner, lat_k, lon_k, out,
    v_innov, v_frac, v_cell, v_owner, v_latk, v_lonk,
    obs, row_table, col_table, total, hsend, hrecv,
    psend, precv, zsend, zrecv, forcing,
    v_anom, fsend, frecv, field, lat_t, weighted, gsend, grecv,
    load_sem, own_sem,
    h_sem, p_sem, z_sem, f_sem, x_sem, ag_sem, core_sem, g_send, g_recv,
):
    mem, lat, lon = lax.axis_index("mem"), lax.axis_index("lat"), lax.axis_index("lon")
    core, y_lo = lax.rem(mem, 2), mem // 2
    z, y_hi = lax.rem(lat, 8), lat // 8
    q = (y_hi * 2 + y_lo) * 4 + lon
    e = y_hi * 4 + lon
    me = lat * 4 + lon
    mate = {"mem": mem + 1 - 2 * core}

    def plane_peer(p):
        y = p // 4
        return {"mem": lax.rem(y, 2) * 2 + core, "lat": (y // 2) * 8 + z, "lon": lax.rem(p, 4)}

    def z_peer(to):
        return {"lat": y_hi * 8 + to}

    def remote(src, dst, send, recv, to):
        return pltpu.make_async_remote_copy(
            src_ref=src, dst_ref=dst, send_sem=send, recv_sem=recv, device_id=to, device_id_type=MESH
        )

    owed, sent = {}, []

    def expect(name, block, count, sems, start=0):
        some = block.at[pl.ds(0, count)]
        owed[name] = remote(some, some, sems.at[0], sems.at[1], mate).wait_recv
        sent.append(remote(some, some, sems.at[0], sems.at[1], mate).wait_send)

    loads = [
        pltpu.make_async_copy(src, dst, load_sem.at[i])
        for i, (src, dst) in enumerate(
            ((innov, v_innov), (frac, v_frac), (cell, v_cell), (owner, v_owner), (anom, v_anom), (lat_k, v_latk), (lon_k, v_lonk))
        )
    ]
    for i, load in enumerate(loads):
        load.start()
        owed[i] = load.wait

    barrier = pltpu.get_barrier_semaphore()

    def greet_plane(s, carry):
        pl.semaphore_signal(barrier, inc=1, device_id=plane_peer(lax.rem(q + s, PLANE)), device_id_type=MESH)
        return carry

    def greet_z(s, carry):
        pl.semaphore_signal(barrier, inc=1, device_id=z_peer(lax.rem(z + s, DEPTH)), device_id_type=MESH)
        return carry

    lax.fori_loop(1, PLANE, greet_plane, 0)
    lax.fori_loop(1, DEPTH, greet_z, 0)
    pl.semaphore_signal(barrier, inc=1, device_id=mate, device_id_type=MESH)

    for i in range(4):
        owed.pop(i)()
    cells = v_cell[...]
    cell_row = ((cells.astype(F32) + 0.5) * (1.0 / COLS)).astype(jnp.int32)
    cell_col = cells - cell_row * COLS
    tile = v_owner[...]
    value, a, b = v_innov[...], v_frac[0:1, :], v_frac[1:2, :]
    obs[0:1, :] = ((tile >> 2) * ROWS + cell_row).astype(F32)
    obs[1:2, :] = ((tile & 3) * COLS + cell_col).astype(F32)
    obs[2:3, :] = value * (1.0 - a)
    obs[3:4, :] = value * a
    obs[4:5, :] = 1.0 - b
    obs[5:6, :] = b

    def rows_of(part):
        at = pl.ds(part * CHUNK, CHUNK)
        row_table[part] = tent_table(obs[0:1, at], obs[2:3, at], obs[3:4, at], LAT)

    def cols_of(part, half, use):
        at, first = pl.ds(part * CHUNK, CHUNK), (half * HALF).astype(F32)
        col_table[use] = tent_table(obs[1:2, at] - first, obs[4:5, at], obs[5:6, at], HALF)

    def spread(part, use):
        return lax.dot_general(
            row_table[part], col_table[use], (((1,), (1,)), ((), ())), preferred_element_type=F32
        )

    owed.pop(4)()

    def pack(m, carry):
        for k in range(LEVELS):
            block = v_anom[m, k].astype(F32)
            tail = block[:, 128:192]
            fsend[lax.rem(m, 8), m // 8, k] = jnp.concatenate(
                [
                    block[:, 0:128],
                    jnp.concatenate([tail[0:8], tail[8:16]], axis=1),
                    jnp.concatenate([tail[16:20], tail[20:24]], axis=1),
                ],
                axis=0,
            ).astype(BF16)
        return carry

    lax.fori_loop(0, 16, pack, 0, unroll=2)

    rows_of(0)
    cols_of(0, 1 - core, 0)
    other = spread(0, 0)
    for p in range(PLANE):
        hsend[p] = other[ROWS * p : ROWS * (p + 1), :].astype(BF16)

    pl.semaphore_wait(barrier, PLANE - 1 + DEPTH - 1 + 1)
    swap = remote(hsend, hrecv, h_sem.at[0], h_sem.at[1], mate)
    swap.start()
    owed["swap"] = swap.wait_recv
    sent.append(swap.wait_send)

    offs = (4, 3, -3, 2, -2, 1, -1)

    def first_leg(leg, slots):
        for i in slots:
            to = lax.rem(z - offs[i - 1] + DEPTH, DEPTH)
            remote(fsend.at[to], frecv.at[i], f_sem.at[leg, 0], f_sem.at[leg, 1], z_peer(to)).start()
        expect("f%d" % leg, fsend, len(slots), f_sem.at[leg])

    first_leg(0, (1, 2, 3))
    own_f = pltpu.make_async_copy(fsend.at[z], frecv.at[0], own_sem.at[0])
    own_f.start()
    owed["own_f"] = own_f.wait

    cols_of(0, core, 1)
    total[...] = spread(0, 1)
    owed.pop("swap")()

    for p in range(PLANE):
        psend[p] = (total[ROWS * p : ROWS * (p + 1), :] + hrecv[p].astype(F32)).astype(BF16)

    def send_p(s, carry):
        to = lax.rem(q + s, PLANE)
        remote(psend.at[to], precv.at[q], p_sem.at[0], p_sem.at[1], plane_peer(to)).start()
        return carry

    lax.fori_loop(1, PLANE, send_p, 0)
    expect("p", psend, PLANE - 1, p_sem)

    owed.pop(5)()
    lat_t[...] = v_latk[...].astype(F32).T.astype(BF16)

    owed.pop("p")()
    band = total[pl.ds(pl.multiple_of(q * ROWS, 8), ROWS), :] + hrecv[q].astype(F32)
    for s in range(1, PLANE):
        band = band + precv[lax.rem(q + s, PLANE)].astype(F32)

    zsend[...] = band.astype(BF16)

    def send_z(s, carry):
        to = lax.rem(z + s, DEPTH)
        remote(zsend, zrecv.at[z], z_sem.at[0], z_sem.at[1], z_peer(to)).start()
        return carry

    lax.fori_loop(1, DEPTH, send_z, 0)
    expect("z", zrecv, DEPTH - 1, z_sem)
    first_leg(1, (4, 5, 6, 7))

    def second_leg(half):
        slots = pl.ds(4 * half, 4)
        for i in range(1, 8):
            to = lax.rem(e + i, 8)
            to_y, to_x = to // 4, lax.rem(to, 4)
            remote(
                frecv.at[slots, to_y, to_x], field.at[e, slots], x_sem.at[half, 0], x_sem.at[half, 1],
                {"lat": to_y * 8 + z, "lon": to_x},
            ).start()
        some = field.at[pl.ds(0, 7), pl.ds(0, 4)]
        copy = remote(some, some, x_sem.at[half, 0], x_sem.at[half, 1], mate)
        owed["x%d" % half] = copy.wait_recv
        sent.append(copy.wait_send)

    owed.pop("f0")()
    owed.pop("own_f")()
    second_leg(0)

    owed.pop("z")()
    for s in range(1, DEPTH):
        band = band + zrecv[lax.rem(z + s, DEPTH)].astype(F32)
    forcing[core, q] = band.astype(BF16)

    def send_ag(s, carry):
        to = lax.rem(q + s, PLANE)
        remote(forcing.at[core, q], forcing.at[core, q], ag_sem.at[0], ag_sem.at[1], plane_peer(to)).start()
        return carry

    lax.fori_loop(1, PLANE, send_ag, 0)
    expect("ag", psend, PLANE - 1, ag_sem)
    owed.pop("f1")()
    second_leg(1)
    own_x = pltpu.make_async_copy(frecv.at[:, y_hi, lon], field.at[e], own_sem.at[1])
    own_x.start()
    owed["own_x"] = own_x.wait
    owed.pop("ag")()
    halves = remote(forcing.at[core], forcing.at[core], core_sem.at[0], core_sem.at[1], mate)
    halves.start()
    owed["half"] = halves.wait_recv
    sent.append(halves.wait_send)

    owed.pop("half")()
    owed.pop("x0")()
    owed.pop("x1")()
    owed.pop("own_x")()
    owed.pop(6)()

    for t in range(DEPTH):
        pair = []
        for band_at in (2 * t, 2 * t + 1):
            y, ahead = band_at // 8, lax.rem(band_at % 8 - z + DEPTH, DEPTH)
            slot = lax.rem(jnp.maximum(2 * ahead - 7, 8 - 2 * ahead), DEPTH)
            row = jnp.concatenate([unpack(field[y * 4 + x, slot].astype(F32)) for x in range(4)], axis=1)
            factor = jnp.concatenate([forcing[0, band_at], forcing[1, band_at]], axis=1).astype(F32)
            pair.append(row * factor)
        weighted[2 * ROWS * t : 2 * ROWS * (t + 1), :] = jnp.concatenate(pair, axis=0).astype(BF16)

    low_lanes = lax.broadcasted_iota(jnp.int32, (8, 128), 1) < 64
    low_wide = lax.broadcasted_iota(jnp.int32, (ROWS, 128), 1) < 64

    for h in range(4):
        mixed = jnp.dot(lat_t[LAT // 4 * h : LAT // 4 * (h + 1), :], weighted[...], preferred_element_type=F32)
        high = mixed.astype(BF16)
        both = jnp.concatenate([high, (mixed - high.astype(F32)).astype(BF16)], axis=0)
        both = jnp.dot(both, v_lonk[...], preferred_element_type=F32)
        grad = both[: LAT // 4] + both[LAT // 4 :]
        for i in range(4):
            for pair_at in range(2):
                t0, t1, t2 = (
                    grad[ROWS * i : ROWS * (i + 1), 384 * pair_at + 128 * j : 384 * pair_at + 128 * (j + 1)]
                    for j in range(3)
                )
                r1, r2 = pltpu.roll(t1, 64, 1), pltpu.roll(t2, 64, 1)
                for odd, (main, low, high) in enumerate(
                    ((t0, t1, r1), (jnp.where(low_wide, r1, r2), r2, t2))
                ):
                    eight = jnp.where(low_lanes, low[0:8], high[8:16])
                    four = jnp.where(low_lanes, low[16:24], pltpu.roll(high[16:24], 4, 0))
                    gsend[(4 * h + i) * 4 + 2 * pair_at + odd] = jnp.concatenate(
                        [main, eight, four[0:4]], axis=0
                    ).astype(BF16)

        def send_g(s, carry):
            to_lat = 4 * h + lax.rem(z + s // 4, 4)
            to_lon = lax.rem(lon + s, 4)
            to = to_lat * 4 + to_lon

            @pl.when(to != me)
            def _():
                remote(
                    gsend.at[to], grecv.at[me], g_send, g_recv.at[lat], {"lat": to_lat, "lon": to_lon}
                ).start()

            return carry

        lax.fori_loop(0, 16, send_g, 0)

    own_g = pltpu.make_async_copy(gsend.at[me], grecv.at[me], own_sem.at[2])
    own_g.start()
    own_g.wait()

    def take(s, carry):
        at = lax.rem(lat + s, 16)

        @pl.when(s == 0)
        def _():
            remote(grecv.at[pl.ds(0, 3)], grecv.at[pl.ds(0, 3)], g_send, g_recv.at[at], mate).wait_recv()

        @pl.when(s != 0)
        def _():
            remote(grecv.at[pl.ds(0, 4)], grecv.at[pl.ds(0, 4)], g_send, g_recv.at[at], mate).wait_recv()

        for k in range(LEVELS):
            out[at, k] = unpack(grecv[at * 4 + k].astype(F32)).astype(BF16)
        return carry

    lax.fori_loop(0, 16, take, 0)

    some = gsend.at[pl.ds(0, GROUP - 1)]
    remote(some, some, g_send, p_sem.at[1], mate).wait_send()
    for wait in sent:
        wait()


def shards(anomalies, innovation, corner_frac, corner_cell, cell_owner, latitude_kernel, longitude_kernel):
    dma = pltpu.SemaphoreType.DMA
    return pl.pallas_call(
        kernel,
        out_shape=pltpu.VMEM(anomalies.shape, BF16),
        in_specs=[pl.BlockSpec(memory_space=pltpu.HBM)] * 7,
        out_specs=pl.BlockSpec(memory_space=pltpu.VMEM),
        scratch_shapes=[
            pltpu.VMEM((1, OBS), F32),
            pltpu.VMEM((2, OBS), F32),
            pltpu.VMEM((1, OBS), jnp.int32),
            pltpu.VMEM((1, OBS), jnp.int32),
            pltpu.VMEM((LAT, LAT), BF16),
            pltpu.VMEM((LON, LON), BF16),
            pltpu.VMEM((8, OBS), F32),
            pltpu.VMEM((1, LAT, CHUNK), BF16),
            pltpu.VMEM((2, HALF, CHUNK), BF16),
            pltpu.VMEM((LAT, HALF), F32),
            pltpu.VMEM((PLANE, ROWS, HALF), BF16),
            pltpu.VMEM((PLANE, ROWS, HALF), BF16),
            pltpu.VMEM((PLANE, ROWS, HALF), BF16),
            pltpu.VMEM((PLANE, ROWS, HALF), BF16),
            pltpu.VMEM((ROWS, HALF), BF16),
            pltpu.VMEM((DEPTH, ROWS, HALF), BF16),
            pltpu.VMEM((2, PLANE, ROWS, HALF), BF16),
            pltpu.VMEM((16, LEVELS, ROWS, COLS), BF16),
            pltpu.VMEM((DEPTH, 2, LEVELS, PACKED, 128), BF16),
            pltpu.VMEM((DEPTH, 2, LEVELS, PACKED, 128), BF16),
            pltpu.VMEM((8, DEPTH, PACKED, 128), BF16),
            pltpu.VMEM((LAT, LAT), BF16),
            pltpu.VMEM((LAT, LON), BF16),
            pltpu.VMEM((GROUP, PACKED, 128), BF16),
            pltpu.VMEM((GROUP, PACKED, 128), BF16),
            dma((7,)),
            dma((3,)),
            dma((2,)),
            dma((2,)),
            dma((2,)),
            dma((2, 2)),
            dma((2, 2)),
            dma((2,)),
            dma((2,)),
            dma,
            dma((16,)),
        ],
        compiler_params=pltpu.CompilerParams(
            collective_id=0, has_side_effects=True, vmem_limit_bytes=60 * 2**20
        ),
    )(*(
        pltpu.with_memory_space_constraint(x, pltpu.HBM)
        for x in (
            anomalies,
            innovation.reshape(1, OBS),
            corner_frac,
            corner_cell.reshape(1, OBS),
            cell_owner.reshape(1, OBS),
            latitude_kernel,
            longitude_kernel,
        )
    ))


def solution(mesh):
    placed = (
        P("mem", None, "lat", "lon"),
        P(("mem", "lat", "lon")),
        P(None, ("mem", "lat", "lon")),
        P(("mem", "lat", "lon")),
        P(("mem", "lat", "lon")),
        P(),
        P(),
    )
    return jax.shard_map(
        shards, mesh=mesh, in_specs=placed, out_specs=P("mem", None, "lat", "lon"), check_vma=False
    )
```

```python
import functools

import jax
import jax.numpy as jnp
from jax import lax
from jax.experimental import pallas as pl
from jax.experimental.pallas import tpu as pltpu
from jax.sharding import PartitionSpec as P

MESH = pl.DeviceIdType.MESH
F32 = jnp.float32
BF16 = jnp.bfloat16

LEVELS, ROWS, COLS = 4, 24, 192
LAT, LON, OBS = 384, 768, 4096
HALF = LON // 2
PLANE, DEPTH, GROUP = 16, 8, 64
CHUNK = 4096
PACKED = 36


def tent_table(index, low, high, count):
    width = index.shape[1]
    low, high = low.astype(BF16), high.astype(BF16)
    rows = lax.broadcasted_iota(jnp.int32, (128, width), 0).astype(F32).astype(BF16)
    parts = []
    for base in range(0, count, 128):
        at = (index - base).astype(BF16)
        after = (index - (base - 1)).astype(BF16)
        parts.append(jnp.where(rows == at, low, jnp.where(rows == after, high, BF16(0))))
    return jnp.concatenate(parts, axis=0)


def unpack(packed):
    eight, four = packed[24:32], packed[32:36]
    tail = jnp.concatenate([eight[:, 0:64], eight[:, 64:128], four[:, 0:64], four[:, 64:128]], axis=0)
    return jnp.concatenate([packed[0:24], tail], axis=1)


def kernel(
    anom, innov, frac, cell, owner, lat_k, lon_k, out,
    v_innov, v_frac, v_cell, v_owner, v_latk, v_lonk,
    obs, row_table, col_table, total, hsend, hrecv,
    psend, precv, zsend, zrecv, forcing,
    v_anom, fsend, frecv, field, lat_t, weighted, gsend, grecv,
    load_sem, own_sem,
    h_sem, p_sem, z_sem, f_sem, x_sem, ag_sem, core_sem, g_send, g_recv,
):
    mem, lat, lon = lax.axis_index("mem"), lax.axis_index("lat"), lax.axis_index("lon")
    core, y_lo = lax.rem(mem, 2), mem // 2
    z, y_hi = lax.rem(lat, 8), lat // 8
    q = (y_hi * 2 + y_lo) * 4 + lon
    e = y_hi * 4 + lon
    me = lat * 4 + lon
    mate = {"mem": mem + 1 - 2 * core}

    def plane_peer(p):
        y = p // 4
        return {"mem": lax.rem(y, 2) * 2 + core, "lat": (y // 2) * 8 + z, "lon": lax.rem(p, 4)}

    def far_first(s):
        s = s - 1 + s // 11
        return lax.rem(q // 4 + 2 + s // 4, 4) * 4 + lax.rem(lon + 2 + s, 4)

    def z_peer(to):
        return {"lat": y_hi * 8 + to}

    def remote(src, dst, send, recv, to):
        return pltpu.make_async_remote_copy(
            src_ref=src, dst_ref=dst, send_sem=send, recv_sem=recv, device_id=to, device_id_type=MESH
        )

    owed, sent = {}, []

    def expect(name, block, count, sems, start=0):
        some = block.at[pl.ds(0, count)]
        owed[name] = remote(some, some, sems.at[0], sems.at[1], mate).wait_recv
        sent.append(remote(some, some, sems.at[0], sems.at[1], mate).wait_send)

    loads = [
        pltpu.make_async_copy(src, dst, load_sem.at[i])
        for i, (src, dst) in enumerate(
            ((innov, v_innov), (frac, v_frac), (cell, v_cell), (owner, v_owner), (anom, v_anom), (lat_k, v_latk), (lon_k, v_lonk))
        )
    ]
    for i, load in enumerate(loads):
        load.start()
        owed[i] = load.wait

    barrier = pltpu.get_barrier_semaphore()

    def greet_plane(s, carry):
        pl.semaphore_signal(barrier, inc=1, device_id=plane_peer(lax.rem(q + s, PLANE)), device_id_type=MESH)
        return carry

    def greet_z(s, carry):
        pl.semaphore_signal(barrier, inc=1, device_id=z_peer(lax.rem(z + s, DEPTH)), device_id_type=MESH)
        return carry

    lax.fori_loop(1, PLANE, greet_plane, 0)
    lax.fori_loop(1, DEPTH, greet_z, 0)
    pl.semaphore_signal(barrier, inc=1, device_id=mate, device_id_type=MESH)

    for i in range(4):
        owed.pop(i)()
    cells = v_cell[...]
    cell_row = ((cells.astype(F32) + 0.5) * (1.0 / COLS)).astype(jnp.int32)
    cell_col = cells - cell_row * COLS
    tile = v_owner[...]
    value, a, b = v_innov[...], v_frac[0:1, :], v_frac[1:2, :]
    obs[0:1, :] = ((tile >> 2) * ROWS + cell_row).astype(F32)
    obs[1:2, :] = ((tile & 3) * COLS + cell_col).astype(F32)
    obs[2:3, :] = value * (1.0 - a)
    obs[3:4, :] = value * a
    obs[4:5, :] = 1.0 - b
    obs[5:6, :] = b

    def rows_of(part):
        at = pl.ds(part * CHUNK, CHUNK)
        row_table[part] = tent_table(obs[0:1, at], obs[2:3, at], obs[3:4, at], LAT)

    def cols_of(part, half, use):
        at, first = pl.ds(part * CHUNK, CHUNK), (half * HALF).astype(F32)
        col_table[use] = tent_table(obs[1:2, at] - first, obs[4:5, at], obs[5:6, at], HALF)

    def spread(part, use):
        return lax.dot_general(
            row_table[part], col_table[use], (((1,), (1,)), ((), ())), preferred_element_type=F32
        )

    owed.pop(4)()

    def pack(m, carry):
        for k in range(LEVELS):
            block = v_anom[m, k].astype(F32)
            tail = block[:, 128:192]
            fsend[lax.rem(m, 8), m // 8, k] = jnp.concatenate(
                [
                    block[:, 0:128],
                    jnp.concatenate([tail[0:8], tail[8:16]], axis=1),
                    jnp.concatenate([tail[16:20], tail[20:24]], axis=1),
                ],
                axis=0,
            ).astype(BF16)
        return carry

    lax.fori_loop(0, 16, pack, 0, unroll=2)

    rows_of(0)
    cols_of(0, 1 - core, 0)
    other = spread(0, 0)
    for p in range(PLANE):
        hsend[p] = other[ROWS * p : ROWS * (p + 1), :].astype(BF16)

    pl.semaphore_wait(barrier, PLANE - 1 + DEPTH - 1 + 1)
    swap = remote(hsend, hrecv, h_sem.at[0], h_sem.at[1], mate)
    swap.start()
    owed["swap"] = swap.wait_recv
    sent.append(swap.wait_send)

    offs = (4, 3, -3, 2, -2, 1, -1)

    def first_leg(leg, slots):
        for i in slots:
            to = lax.rem(z - offs[i - 1] + DEPTH, DEPTH)
            remote(fsend.at[to], frecv.at[i], f_sem.at[leg, 0], f_sem.at[leg, 1], z_peer(to)).start()
        expect("f%d" % leg, fsend, len(slots), f_sem.at[leg])

    first_leg(0, (1, 2, 3))
    own_f = pltpu.make_async_copy(fsend.at[z], frecv.at[0], own_sem.at[0])
    own_f.start()
    owed["own_f"] = own_f.wait

    cols_of(0, core, 1)
    total[...] = spread(0, 1)
    owed.pop("swap")()

    for p in range(PLANE):
        psend[p] = (total[ROWS * p : ROWS * (p + 1), :] + hrecv[p].astype(F32)).astype(BF16)

    def send_p(s, carry):
        to = far_first(s)
        remote(psend.at[to], precv.at[q], p_sem.at[0], p_sem.at[1], plane_peer(to)).start()
        return carry

    lax.fori_loop(1, PLANE, send_p, 0)
    expect("p", psend, PLANE - 1, p_sem)

    owed.pop(5)()
    lat_t[...] = v_latk[...].astype(F32).T.astype(BF16)

    owed.pop("p")()
    band = total[pl.ds(pl.multiple_of(q * ROWS, 8), ROWS), :] + hrecv[q].astype(F32)
    for s in range(1, PLANE):
        band = band + precv[lax.rem(q + s, PLANE)].astype(F32)

    zsend[...] = band.astype(BF16)

    def send_z(s, carry):
        to = lax.rem(z + s, DEPTH)
        remote(zsend, zrecv.at[z], z_sem.at[0], z_sem.at[1], z_peer(to)).start()
        return carry

    lax.fori_loop(1, DEPTH, send_z, 0)
    expect("z", zrecv, DEPTH - 1, z_sem)
    first_leg(1, (4, 5, 6, 7))

    def second_leg(half):
        slots = pl.ds(4 * half, 4)
        for i in range(1, 8):
            to = lax.rem(e + i, 8)
            to_y, to_x = to // 4, lax.rem(to, 4)
            remote(
                frecv.at[slots, to_y, to_x], field.at[e, slots], x_sem.at[half, 0], x_sem.at[half, 1],
                {"lat": to_y * 8 + z, "lon": to_x},
            ).start()
        some = field.at[pl.ds(0, 7), pl.ds(0, 4)]
        copy = remote(some, some, x_sem.at[half, 0], x_sem.at[half, 1], mate)
        owed["x%d" % half] = copy.wait_recv
        sent.append(copy.wait_send)

    owed.pop("f0")()
    owed.pop("own_f")()
    second_leg(0)

    owed.pop("z")()
    for s in range(1, DEPTH):
        band = band + zrecv[lax.rem(z + s, DEPTH)].astype(F32)
    forcing[core, q] = band.astype(BF16)

    def send_ag(s, carry):
        to = far_first(s)
        remote(forcing.at[core, q], forcing.at[core, q], ag_sem.at[0], ag_sem.at[1], plane_peer(to)).start()
        return carry

    lax.fori_loop(1, PLANE, send_ag, 0)
    expect("ag", psend, PLANE - 1, ag_sem)
    owed.pop("f1")()
    second_leg(1)
    own_x = pltpu.make_async_copy(frecv.at[:, y_hi, lon], field.at[e], own_sem.at[1])
    own_x.start()
    owed["own_x"] = own_x.wait
    owed.pop("ag")()
    halves = remote(forcing.at[core], forcing.at[core], core_sem.at[0], core_sem.at[1], mate)
    halves.start()
    owed["half"] = halves.wait_recv
    sent.append(halves.wait_send)

    owed.pop("half")()
    owed.pop("x0")()
    owed.pop("x1")()
    owed.pop("own_x")()
    owed.pop(6)()

    for t in range(DEPTH):
        pair = []
        for band_at in (2 * t, 2 * t + 1):
            y, ahead = band_at // 8, lax.rem(band_at % 8 - z + DEPTH, DEPTH)
            slot = lax.rem(jnp.maximum(2 * ahead - 7, 8 - 2 * ahead), DEPTH)
            row = jnp.concatenate([unpack(field[y * 4 + x, slot].astype(F32)) for x in range(4)], axis=1)
            factor = jnp.concatenate([forcing[0, band_at], forcing[1, band_at]], axis=1).astype(F32)
            pair.append(row * factor)
        weighted[2 * ROWS * t : 2 * ROWS * (t + 1), :] = jnp.concatenate(pair, axis=0).astype(BF16)

    low_lanes = lax.broadcasted_iota(jnp.int32, (8, 128), 1) < 64
    low_wide = lax.broadcasted_iota(jnp.int32, (ROWS, 128), 1) < 64

    for h in range(4):
        mixed = jnp.dot(lat_t[LAT // 4 * h : LAT // 4 * (h + 1), :], weighted[...], preferred_element_type=F32)
        high = mixed.astype(BF16)
        both = jnp.concatenate([high, (mixed - high.astype(F32)).astype(BF16)], axis=0)
        both = jnp.dot(both, v_lonk[...], preferred_element_type=F32)
        grad = both[: LAT // 4] + both[LAT // 4 :]
        for i in range(4):
            for pair_at in range(2):
                t0, t1, t2 = (
                    grad[ROWS * i : ROWS * (i + 1), 384 * pair_at + 128 * j : 384 * pair_at + 128 * (j + 1)]
                    for j in range(3)
                )
                r1, r2 = pltpu.roll(t1, 64, 1), pltpu.roll(t2, 64, 1)
                for odd, (main, low, high) in enumerate(
                    ((t0, t1, r1), (jnp.where(low_wide, r1, r2), r2, t2))
                ):
                    eight = jnp.where(low_lanes, low[0:8], high[8:16])
                    four = jnp.where(low_lanes, low[16:24], pltpu.roll(high[16:24], 4, 0))
                    gsend[(4 * h + i) * 4 + 2 * pair_at + odd] = jnp.concatenate(
                        [main, eight, four[0:4]], axis=0
                    ).astype(BF16)

        def send_g(s, carry):
            to_lat = 4 * h + lax.rem(z + s // 4, 4)
            to_lon = lax.rem(lon + s, 4)
            to = to_lat * 4 + to_lon

            @pl.when(to != me)
            def _():
                remote(
                    gsend.at[to], grecv.at[me], g_send, g_recv.at[lat], {"lat": to_lat, "lon": to_lon}
                ).start()

            return carry

        lax.fori_loop(0, 16, send_g, 0)

    own_g = pltpu.make_async_copy(gsend.at[me], grecv.at[me], own_sem.at[2])
    own_g.start()
    own_g.wait()

    def take(s, carry):
        at = lax.rem(lat + s, 16)

        @pl.when(s == 0)
        def _():
            remote(grecv.at[pl.ds(0, 3)], grecv.at[pl.ds(0, 3)], g_send, g_recv.at[at], mate).wait_recv()

        @pl.when(s != 0)
        def _():
            remote(grecv.at[pl.ds(0, 4)], grecv.at[pl.ds(0, 4)], g_send, g_recv.at[at], mate).wait_recv()

        for k in range(LEVELS):
            out[at, k] = unpack(grecv[at * 4 + k].astype(F32)).astype(BF16)
        return carry

    lax.fori_loop(0, 16, take, 0)

    some = gsend.at[pl.ds(0, GROUP - 1)]
    remote(some, some, g_send, p_sem.at[1], mate).wait_send()
    for wait in sent:
        wait()


def shards(anomalies, innovation, corner_frac, corner_cell, cell_owner, latitude_kernel, longitude_kernel):
    dma = pltpu.SemaphoreType.DMA
    return pl.pallas_call(
        kernel,
        out_shape=pltpu.VMEM(anomalies.shape, BF16),
        in_specs=[pl.BlockSpec(memory_space=pltpu.HBM)] * 7,
        out_specs=pl.BlockSpec(memory_space=pltpu.VMEM),
        scratch_shapes=[
            pltpu.VMEM((1, OBS), F32),
            pltpu.VMEM((2, OBS), F32),
            pltpu.VMEM((1, OBS), jnp.int32),
            pltpu.VMEM((1, OBS), jnp.int32),
            pltpu.VMEM((LAT, LAT), BF16),
            pltpu.VMEM((LON, LON), BF16),
            pltpu.VMEM((8, OBS), F32),
            pltpu.VMEM((1, LAT, CHUNK), BF16),
            pltpu.VMEM((2, HALF, CHUNK), BF16),
            pltpu.VMEM((LAT, HALF), F32),
            pltpu.VMEM((PLANE, ROWS, HALF), BF16),
            pltpu.VMEM((PLANE, ROWS, HALF), BF16),
            pltpu.VMEM((PLANE, ROWS, HALF), BF16),
            pltpu.VMEM((PLANE, ROWS, HALF), BF16),
            pltpu.VMEM((ROWS, HALF), BF16),
            pltpu.VMEM((DEPTH, ROWS, HALF), BF16),
            pltpu.VMEM((2, PLANE, ROWS, HALF), BF16),
            pltpu.VMEM((16, LEVELS, ROWS, COLS), BF16),
            pltpu.VMEM((DEPTH, 2, LEVELS, PACKED, 128), BF16),
            pltpu.VMEM((DEPTH, 2, LEVELS, PACKED, 128), BF16),
            pltpu.VMEM((8, DEPTH, PACKED, 128), BF16),
            pltpu.VMEM((LAT, LAT), BF16),
            pltpu.VMEM((LAT, LON), BF16),
            pltpu.VMEM((GROUP, PACKED, 128), BF16),
            pltpu.VMEM((GROUP, PACKED, 128), BF16),
            dma((7,)),
            dma((3,)),
            dma((2,)),
            dma((2,)),
            dma((2,)),
            dma((2, 2)),
            dma((2, 2)),
            dma((2,)),
            dma((2,)),
            dma,
            dma((16,)),
        ],
        compiler_params=pltpu.CompilerParams(
            collective_id=0, has_side_effects=True, vmem_limit_bytes=60 * 2**20
        ),
    )(*(
        pltpu.with_memory_space_constraint(x, pltpu.HBM)
        for x in (
            anomalies,
            innovation.reshape(1, OBS),
            corner_frac,
            corner_cell.reshape(1, OBS),
            cell_owner.reshape(1, OBS),
            latitude_kernel,
            longitude_kernel,
        )
    ))


def solution(mesh):
    placed = (
        P("mem", None, "lat", "lon"),
        P(("mem", "lat", "lon")),
        P(None, ("mem", "lat", "lon")),
        P(("mem", "lat", "lon")),
        P(("mem", "lat", "lon")),
        P(),
        P(),
    )
    return jax.shard_map(
        shards, mesh=mesh, in_specs=placed, out_specs=P("mem", None, "lat", "lon"), check_vma=False
    )
```
